768 devices in a mesh: outer: 96 (over z_lo, y, core), inner: 8 (over z_hi, x).
Axes of the slice: x: 4, y: 8, z: 12 (z_hi: 2, z_lo: 6; z = z_hi * 6 + z_lo), core: 2. Of those that a mesh axis runs over, the one named last changes fastest.
Arguments:
- tokens: bfloat16 [196608, 8192], P(('outer', 'inner')), may hold values from -6 to 6
- cotangent: bfloat16 [196608, 48], P(('outer', 'inner')), may hold values from -0.0134887695 to 0.0134887695
- w_codes: bfloat16 [48, 64, 128], P(None, 'inner'), may hold values from -1 to 1
- w_scales: float32 [48, 64], P(None, 'inner'), may hold values from 0.01 to 0.04
Outputs:
- grad_shard: float32 [3072, 128], P(('outer', 'inner'))
The draws below stay inside these ranges and needn't reach their ends.
All inputs are finite; a program needn't handle non-finite values.
Results may differ from the reference program's by a relative error of at most 0.018.
Values may be sent and summed in bfloat16 or wider, within the bound.
No kernel may reach another device: no remote copies, remote signals or barrier semaphores. Data moves between devices by JAX's collectives and lax.ppermute only.
A program may use at most 32 MiB of HBM per device.

```python
import math
import jax
import jax.numpy as jnp
from jax import lax

D = 8192
BR = 48
BLOCK = 128
TOK_DEV = 256
TOKENS = 196608
NBLK = 64
BLOCKS = 3072
N_OUTER = 96
N_INNER = 8


def level_of(rng, extent, cuts, smallest, top_value):
    loudness = 1.0
    for dim, parts in cuts:
        draws = jax.random.uniform(jax.random.fold_in(jax.random.fold_in(rng, 6), dim), (parts,), jnp.float32, smallest / len(cuts), top_value / len(cuts))
        loudness = loudness * jnp.repeat(jnp.exp(draws), extent[dim] // parts).reshape((-1,) + (1,) * (len(extent) - 1 - dim))
    return loudness


def noise(own_key, extent, scale, limit, shards=(), kind=jnp.bfloat16):
    level = level_of(own_key, extent, shards, -0.22, 0.18) if shards else 1.0
    array = jax.random.normal(own_key, extent, jnp.float32) * scale * level
    return jnp.minimum(jnp.maximum(array, -limit), limit).astype(kind)


def setup_inputs(seed: int = 0) -> dict:
    key_of = jax.random.split(jax.random.key(seed), 5)
    return {
        "tokens": noise(key_of[0], (TOKENS, D), 1.0, 6.0, ((0, 768),)),
        "cotangent": noise(key_of[1], (TOKENS, BR), (TOKENS ** -0.5), 0.0134887695, ((0, 768),)),
        "w_codes": jnp.clip(jax.random.uniform(key_of[2], (BR, NBLK, BLOCK), jnp.float32, -1.0, 1.0) * level_of(key_of[2], (BR, NBLK, BLOCK), ((1, 8),), -0.4, 0.0), -1.0, 1.0).astype(jnp.bfloat16),
        "w_scales": jnp.clip(jnp.exp(math.log(0.04) - 1.3862944 * jax.random.uniform(key_of[3], (BR, NBLK), jnp.float32) ** level_of(key_of[3], (BR, NBLK), ((1, 8),), -0.2, 0.2)), 0.01, 0.04),
    }


def round_trip(values):
    return lax.optimization_barrier(values.astype(jnp.bfloat16)).astype(jnp.float32)


def slope(pre):
    sig = jax.nn.sigmoid(pre)
    return sig * (1.0 + pre * (1.0 - sig))


def reference(tokens, cotangent, w_codes, w_scales):
    per_dev = BLOCKS // (N_OUTER * N_INNER)
    weight = (w_codes.astype(jnp.float32) * w_scales[..., None]).astype(jnp.bfloat16).reshape(BR, D)
    tok_all = tokens.reshape(N_OUTER, N_INNER, TOK_DEV, D)
    cot_all = cotangent.reshape(N_OUTER, N_INNER, TOK_DEV, BR)

    def member(carry, pair):
        tok_dev, cot_dev = pair
        pre = lax.dot_general(tok_dev, weight, (((1,), (1,)), ((), ())), preferred_element_type=jnp.float32)
        delta = (cot_dev.astype(jnp.float32) * slope(pre)).astype(jnp.bfloat16)
        local_grad = lax.dot_general(delta, tok_dev, (((0,), (0,)), ((), ())), preferred_element_type=jnp.float32)
        return carry + round_trip(local_grad.reshape(N_OUTER, N_INNER, per_dev, BLOCK)), None

    def group(carry, pair):
        zeros = jnp.zeros((N_OUTER, N_INNER, per_dev, BLOCK), jnp.float32)
        partial_value, _ = lax.scan(member, zeros, pair)
        return carry + round_trip(partial_value), None

    total, _ = lax.scan(group, jnp.zeros((N_OUTER, N_INNER, per_dev, BLOCK), jnp.float32), (tok_all, cot_all))
    return total.reshape(BLOCKS, BLOCK)
```

```python
import jax
import jax.numpy as jnp
from jax import lax
from jax.sharding import Mesh, PartitionSpec as P

BLOCK = 128
Z_LO, Y, CORE, Z_HI, X = 6, 8, 2, 2, 4
ROWS = 48
HALF_ROWS = ROWS // CORE
SHARD = 1024
PIECE = 512


def slope(pre):
    sig = jax.nn.sigmoid(pre)
    return sig * (1.0 + pre * (1.0 - sig))


def gather_weight(w_codes, w_scales):
    core = lax.axis_index("core")
    z_hi = lax.axis_index("z_hi")
    codes = lax.dynamic_slice_in_dim(w_codes, core * HALF_ROWS, HALF_ROWS, 0)
    scales = lax.dynamic_slice_in_dim(w_scales, core * HALF_ROWS, HALF_ROWS, 0)
    mine = (codes.astype(jnp.float32) * scales[..., None]).astype(jnp.bfloat16)
    mine = mine.reshape(HALF_ROWS, SHARD)
    mirror = [
        (lo * Z_HI + hi, (Z_LO - 1 - lo) * Z_HI + (1 - hi))
        for lo in range(Z_LO)
        for hi in range(Z_HI)
    ]
    other = lax.ppermute(mine, ("z_lo", "z_hi"), mirror)
    first = jnp.where(z_hi == 0, mine, other)
    second = jnp.where(z_hi == 0, other, mine)
    both = jnp.stack([first, second])
    return lax.all_gather(both, "x", axis=0)


def on_device(tokens, cotangent, w_codes, w_scales):
    core = lax.axis_index("core")
    swap = [(0, 1), (1, 0)]
    my_rows = gather_weight(w_codes, w_scales)
    their_rows = lax.ppermute(my_rows, "core", swap)
    rows = jnp.where(
        core == 0, jnp.stack([my_rows, their_rows]), jnp.stack([their_rows, my_rows])
    )
    weight = rows.transpose(0, 3, 2, 1, 4).reshape(ROWS, -1)
    pre = lax.dot_general(
        tokens, weight, (((1,), (1,)), ((), ())), preferred_element_type=jnp.float32
    )
    delta = (cotangent.astype(jnp.float32) * slope(pre)).astype(jnp.bfloat16)
    local_grad = lax.dot_general(
        delta, tokens, (((0,), (0,)), ((), ())), preferred_element_type=jnp.float32
    ).astype(jnp.bfloat16)
    width = local_grad.shape[1] // CORE
    keep = lax.dynamic_slice_in_dim(local_grad, core * width, width, 1)
    give = lax.dynamic_slice_in_dim(local_grad, (1 - core) * width, width, 1)
    got = lax.ppermute(give, "core", swap)
    chip = (keep.astype(jnp.float32) + got.astype(jnp.float32)).astype(jnp.bfloat16)
    by_x = chip.reshape(ROWS, Z_HI, X, PIECE).transpose(2, 0, 1, 3).reshape(X, ROWS, Z_HI * PIECE)
    from_x = lax.all_to_all(by_x, "x", split_axis=0, concat_axis=0, tiled=True)
    row_sum = jnp.sum(from_x.astype(jnp.float32), axis=0).astype(jnp.bfloat16)
    by_yz = row_sum.reshape(ROWS * Z_HI, PIECE // BLOCK, BLOCK)
    from_yz = lax.all_to_all(by_yz, ("z_lo", "y", "z_hi"), split_axis=0, concat_axis=0, tiled=True)
    return jnp.sum(from_yz.astype(jnp.float32), axis=0)


def solution(mesh):
    fine = Mesh(
        mesh.devices.reshape(Z_LO, Y, CORE, Z_HI, X), ("z_lo", "y", "core", "z_hi", "x")
    )
    outer, inner = ("z_lo", "y", "core"), ("z_hi", "x")
    in_specs = (
        P(outer + inner, None),
        P(outer + inner, None),
        P(None, inner, None),
        P(None, inner),
    )
    return jax.shard_map(
        on_device, mesh=fine, in_specs=in_specs, out_specs=P(outer + inner, None), check_vma=False
    )
```

```python
import jax
import jax.numpy as jnp
from jax import lax
from jax.sharding import Mesh, PartitionSpec as P

BLOCK = 128
Z_LO, Y, CORE, Z_HI, X = 6, 8, 2, 2, 4
ROWS = 48
HALF_ROWS = ROWS // CORE
SHARD = 1024
PIECE = 512


def slope(pre):
    sig = jax.nn.sigmoid(pre)
    return sig * (1.0 + pre * (1.0 - sig))


def gather_weight(w_codes, w_scales):
    core = lax.axis_index("core")
    z_hi = lax.axis_index("z_hi")
    codes = lax.dynamic_slice_in_dim(w_codes, core * HALF_ROWS, HALF_ROWS, 0)
    scales = lax.dynamic_slice_in_dim(w_scales, core * HALF_ROWS, HALF_ROWS, 0)
    mine = (codes.astype(jnp.float32) * scales[..., None]).astype(jnp.bfloat16)
    mine = mine.reshape(HALF_ROWS, SHARD)
    shift = [
        (lo * Z_HI + hi, (lo + Z_LO // 2) % Z_LO * Z_HI + (1 - hi))
        for lo in range(Z_LO)
        for hi in range(Z_HI)
    ]
    other = lax.ppermute(mine, ("z_lo", "z_hi"), shift)
    first = jnp.where(z_hi == 0, mine, other)
    second = jnp.where(z_hi == 0, other, mine)
    both = jnp.stack([first, second])
    copies = jnp.broadcast_to(both[None], (X,) + both.shape)
    return lax.all_to_all(copies, "x", split_axis=0, concat_axis=0, tiled=True)


def on_device(tokens, cotangent, w_codes, w_scales):
    core = lax.axis_index("core")
    swap = [(0, 1), (1, 0)]
    my_rows = gather_weight(w_codes, w_scales)
    their_rows = lax.ppermute(my_rows, "core", swap)
    rows = jnp.where(
        core == 0, jnp.stack([my_rows, their_rows]), jnp.stack([their_rows, my_rows])
    )
    weight = rows.transpose(0, 3, 2, 1, 4).reshape(ROWS, -1)
    pre = lax.dot_general(
        tokens, weight, (((1,), (1,)), ((), ())), preferred_element_type=jnp.float32
    )
    delta = (cotangent.astype(jnp.float32) * slope(pre)).astype(jnp.bfloat16)
    local_grad = lax.dot_general(
        delta, tokens, (((0,), (0,)), ((), ())), preferred_element_type=jnp.float32
    ).astype(jnp.bfloat16)
    width = local_grad.shape[1] // CORE
    keep = lax.dynamic_slice_in_dim(local_grad, core * width, width, 1)
    give = lax.dynamic_slice_in_dim(local_grad, (1 - core) * width, width, 1)
    got = lax.ppermute(give, "core", swap)
    chip = (keep.astype(jnp.float32) + got.astype(jnp.float32)).astype(jnp.bfloat16)
    by_yx = chip.reshape(Z_LO, Y, Z_HI, X, PIECE).transpose(1, 3, 0, 2, 4)
    by_yx = by_yx.reshape(Y * X, Z_LO * Z_HI * PIECE // BLOCK, BLOCK)
    from_yx = lax.all_to_all(by_yx, ("y", "x"), split_axis=0, concat_axis=0, tiled=True)
    part = jnp.sum(from_yx.astype(jnp.float32), axis=0).astype(jnp.bfloat16)
    by_z = part.reshape(Z_LO * Z_HI, PIECE // BLOCK, BLOCK)
    from_z = lax.all_to_all(by_z, ("z_lo", "z_hi"), split_axis=0, concat_axis=0, tiled=True)
    return jnp.sum(from_z.astype(jnp.float32), axis=0)


def solution(mesh):
    fine = Mesh(
        mesh.devices.reshape(Z_LO, Y, CORE, Z_HI, X), ("z_lo", "y", "core", "z_hi", "x")
    )
    outer, inner = ("z_lo", "y", "core"), ("z_hi", "x")
    in_specs = (
        P(outer + inner, None),
        P(outer + inner, None),
        P(None, inner, None),
        P(None, inner),
    )
    return jax.shard_map(
        on_device, mesh=fine, in_specs=in_specs, out_specs=P(outer + inner, None), check_vma=False
    )
```

```python
import jax
import jax.numpy as jnp
from jax import lax
from jax.experimental import pallas as pl
from jax.experimental.pallas import tpu as pltpu
from jax.sharding import Mesh, PartitionSpec as P

BLOCK = 128
Z_LO, Y, CORE, Z_HI, X = 6, 8, 2, 2, 4
ROWS = 48
HALF_ROWS = ROWS // CORE
SHARD = 1024
PIECE = 512
PIECE_BLOCKS = PIECE // BLOCK
VMEM = pl.BlockSpec(memory_space=pltpu.VMEM)
HBM = pl.BlockSpec(memory_space=pltpu.HBM)
SMEM = pl.BlockSpec(memory_space=pltpu.SMEM)
SWAP = ((0, 1), (1, 0))


def in_vmem(array):
    return pltpu.with_memory_space_constraint(array, pltpu.VMEM)


def in_hbm(array):
    return pltpu.with_memory_space_constraint(array, pltpu.HBM)


def slope(pre):
    sig = jax.nn.sigmoid(pre)
    return sig * (1.0 + pre * (1.0 - sig))


def prepare_kernel(core_ref, codes_hbm, scales_hbm, mine_ref, codes_ref, scales_ref, sems):
    copies = [
        pltpu.make_async_copy(
            codes_hbm.at[pl.ds(core_ref[0] * HALF_ROWS, HALF_ROWS)], codes_ref, sems.at[0]
        ),
        pltpu.make_async_copy(scales_hbm, scales_ref, sems.at[1]),
    ]
    for copy in copies:
        copy.start()
    for copy in copies:
        copy.wait()
    codes = codes_ref[...].astype(jnp.float32).reshape(HALF_ROWS, SHARD)
    scales = scales_ref[...].T
    scales = jnp.where(core_ref[0] == 0, scales[:HALF_ROWS], scales[HALF_ROWS:])
    for k in range(SHARD // BLOCK):
        block = slice(k * BLOCK, (k + 1) * BLOCK)
        mine_ref[:, block] = (codes[:, block] * scales[:, k : k + 1]).astype(jnp.bfloat16)


def prepare(core, w_codes, w_scales):
    scales = w_scales.T
    return pl.pallas_call(
        prepare_kernel,
        out_shape=jax.ShapeDtypeStruct((HALF_ROWS, SHARD), jnp.bfloat16),
        in_specs=[SMEM, HBM, HBM],
        out_specs=VMEM,
        scratch_shapes=[
            pltpu.VMEM((HALF_ROWS,) + w_codes.shape[1:], w_codes.dtype),
            pltpu.VMEM(scales.shape, scales.dtype),
            pltpu.SemaphoreType.DMA((2,)),
        ],
        compiler_params=pltpu.CompilerParams(vmem_limit_bytes=8 * 2**20),
        name="prepare",
    )(core.reshape(1), in_hbm(w_codes), in_hbm(scales))


def spread_kernel(hi_ref, mine_ref, other_ref, out_ref):
    mine, other = mine_ref[...], other_ref[...]
    low = hi_ref[0] == 0
    first = jnp.where(low, mine, other)
    second = jnp.where(low, other, mine)
    for x in range(X):
        out_ref[x, :, :SHARD] = first
        out_ref[x, :, SHARD:] = second


def spread(z_hi, mine, other):
    return pl.pallas_call(
        spread_kernel,
        out_shape=jax.ShapeDtypeStruct((X, HALF_ROWS, Z_HI * SHARD), jnp.bfloat16),
        in_specs=[SMEM, VMEM, VMEM],
        out_specs=VMEM,
        compiler_params=pltpu.CompilerParams(vmem_limit_bytes=8 * 2**20),
        name="spread",
    )(z_hi.reshape(1), mine, other)


def product(w_ref, tok_ref, hi, pre):
    for x in range(X):
        rows = w_ref[x, :, pl.ds(pl.multiple_of(hi * SHARD, SHARD), SHARD)]
        columns = pl.ds(pl.multiple_of((hi * X + x) * SHARD, SHARD), SHARD)
        pre += lax.dot_general(
            rows, tok_ref[:, columns], (((1,), (1,)), ((), ())), preferred_element_type=jnp.float32
        )
    return pre


def own_kernel(w_ref, tok_hbm, pre_ref, tok_ref, sems):
    def copy(hi):
        columns = pl.ds(pl.multiple_of(hi * X * SHARD, SHARD), X * SHARD)
        return pltpu.make_async_copy(tok_hbm.at[:, columns], tok_ref.at[:, columns], sems.at[hi])

    for hi in range(Z_HI):
        copy(hi).start()

    def step(hi, pre):
        copy(hi).wait()
        return product(w_ref, tok_ref, hi, pre)

    pre_ref[...] = lax.fori_loop(0, Z_HI, step, jnp.zeros(pre_ref.shape, jnp.float32))


def own_rows(weight, tokens):
    return pl.pallas_call(
        own_kernel,
        out_shape=[
            jax.ShapeDtypeStruct((HALF_ROWS, tokens.shape[0]), jnp.float32),
            pltpu.VMEM(tokens.shape, tokens.dtype),
        ],
        in_specs=[VMEM, HBM],
        out_specs=[VMEM] * 2,
        scratch_shapes=[pltpu.SemaphoreType.DMA((Z_HI,))],
        compiler_params=pltpu.CompilerParams(vmem_limit_bytes=8 * 2**20),
        name="own_rows",
    )(weight, in_hbm(tokens))


def grad_kernel(core_ref, w_ref, pre_ref, cot_ref, tok_ref, out_ref):
    mine = pre_ref[...]
    theirs = jnp.zeros_like(mine)
    for hi in range(Z_HI):
        theirs = product(w_ref, tok_ref, hi, theirs)
    first = core_ref[0] == 0
    pre = jnp.concatenate(
        [jnp.where(first, mine, theirs), jnp.where(first, theirs, mine)], axis=0
    )
    delta = (cot_ref[...].astype(jnp.float32) * slope(pre)).astype(jnp.bfloat16)
    for h in range(CORE):
        for hi in range(Z_HI):
            for x in range(X):
                column = ((h * Z_HI + hi) * X + x) * PIECE
                out_ref[h * X + x, :, hi * PIECE : (hi + 1) * PIECE] = jnp.dot(
                    delta,
                    tok_ref[:, column : column + PIECE],
                    preferred_element_type=jnp.float32,
                ).astype(jnp.bfloat16)


def gradient(core, weight, pre, cotangent, tokens):
    return pl.pallas_call(
        grad_kernel,
        out_shape=jax.ShapeDtypeStruct((CORE * X, ROWS, Z_HI * PIECE), jnp.bfloat16),
        in_specs=[SMEM] + [VMEM] * 4,
        out_specs=VMEM,
        compiler_params=pltpu.CompilerParams(vmem_limit_bytes=8 * 2**20),
        name="gradient",
    )(core.reshape(1), weight, pre, cotangent.T, in_vmem(tokens))


def sum_kernel(in_ref, out_ref):
    total = jnp.sum(in_ref[...].astype(jnp.float32), axis=0)
    out_ref[...] = total.reshape(out_ref.shape).astype(jnp.bfloat16)


def sum_peers(parts):
    blocks = ROWS * Z_HI * PIECE_BLOCKS
    return pl.pallas_call(
        sum_kernel,
        out_shape=jax.ShapeDtypeStruct((blocks, BLOCK), jnp.bfloat16),
        in_specs=[VMEM],
        out_specs=VMEM,
        compiler_params=pltpu.CompilerParams(vmem_limit_bytes=8 * 2**20),
        name="sum_peers",
    )(parts)


def on_device(tokens, cotangent, w_codes, w_scales):
    core = lax.axis_index("core")
    z_hi = lax.axis_index("z_hi")

    mine = prepare(core, w_codes, w_scales)
    shift = [
        (lo * Z_HI + hi, (lo + Z_LO // 2) % Z_LO * Z_HI + (1 - hi))
        for lo in range(Z_LO)
        for hi in range(Z_HI)
    ]
    other = lax.ppermute(mine, ("z_lo", "z_hi"), shift)
    copies = spread(z_hi, mine, other)
    half = lax.all_to_all(copies, "x", split_axis=0, concat_axis=0, tiled=True)

    theirs = lax.ppermute(half, "core", SWAP)
    pre, staged = own_rows(half, tokens)
    grad = gradient(core, theirs, pre, cotangent, staged)

    from_x = lax.all_to_all(grad, ("core", "x"), split_axis=0, concat_axis=0, tiled=True)
    by_yz = sum_peers(from_x).reshape(Z_LO * Y * Z_HI, PIECE_BLOCKS, BLOCK)
    from_yz = lax.all_to_all(
        by_yz, ("z_lo", "y", "z_hi"), split_axis=0, concat_axis=0, tiled=True
    )
    return jnp.sum(from_yz.astype(jnp.float32), axis=0)


def solution(mesh):
    fine = Mesh(
        mesh.devices.reshape(Z_LO, Y, CORE, Z_HI, X), ("z_lo", "y", "core", "z_hi", "x")
    )
    outer, inner = ("z_lo", "y", "core"), ("z_hi", "x")
    in_specs = (
        P(outer + inner, None),
        P(outer + inner, None),
        P(None, inner, None),
        P(None, inner),
    )
    return jax.shard_map(
        on_device, mesh=fine, in_specs=in_specs, out_specs=P(outer + inner, None), check_vma=False
    )
```

```python
import jax
import jax.numpy as jnp
from jax import lax
from jax.experimental import pallas as pl
from jax.experimental.pallas import tpu as pltpu
from jax.sharding import Mesh, PartitionSpec as P

BLOCK = 128
Z_LO, Y, CORE, Z_HI, X = 6, 8, 2, 2, 4
ROWS = 48
HALF_ROWS = ROWS // CORE
SHARD = 1024
PIECE = 512
PIECE_BLOCKS = PIECE // BLOCK
VMEM = pl.BlockSpec(memory_space=pltpu.VMEM)
HBM = pl.BlockSpec(memory_space=pltpu.HBM)
SMEM = pl.BlockSpec(memory_space=pltpu.SMEM)
SWAP = ((0, 1), (1, 0))


def in_vmem(array):
    return pltpu.with_memory_space_constraint(array, pltpu.VMEM)


def in_hbm(array):
    return pltpu.with_memory_space_constraint(array, pltpu.HBM)


def slope(pre):
    sig = jax.nn.sigmoid(pre)
    return sig * (1.0 + pre * (1.0 - sig))


def prepare_kernel(core_ref, codes_hbm, scales_hbm, mine_ref, codes_ref, scales_ref, sems):
    copies = [
        pltpu.make_async_copy(
            codes_hbm.at[pl.ds(core_ref[0] * HALF_ROWS, HALF_ROWS)], codes_ref, sems.at[0]
        ),
        pltpu.make_async_copy(scales_hbm, scales_ref, sems.at[1]),
    ]
    for copy in copies:
        copy.start()
    for copy in copies:
        copy.wait()
    codes = codes_ref[...].astype(jnp.float32).reshape(HALF_ROWS, SHARD)
    scales = scales_ref[...].T
    scales = jnp.where(core_ref[0] == 0, scales[:HALF_ROWS], scales[HALF_ROWS:])
    for k in range(SHARD // BLOCK):
        block = slice(k * BLOCK, (k + 1) * BLOCK)
        mine_ref[:, block] = (codes[:, block] * scales[:, k : k + 1]).astype(jnp.bfloat16)


def prepare(core, w_codes, w_scales):
    scales = w_scales.T
    return pl.pallas_call(
        prepare_kernel,
        out_shape=jax.ShapeDtypeStruct((HALF_ROWS, SHARD), jnp.bfloat16),
        in_specs=[SMEM, HBM, HBM],
        out_specs=VMEM,
        scratch_shapes=[
            pltpu.VMEM((HALF_ROWS,) + w_codes.shape[1:], w_codes.dtype),
            pltpu.VMEM(scales.shape, scales.dtype),
            pltpu.SemaphoreType.DMA((2,)),
        ],
        compiler_params=pltpu.CompilerParams(vmem_limit_bytes=8 * 2**20),
        name="prepare",
    )(core.reshape(1), in_hbm(w_codes), in_hbm(scales))


def spread_kernel(hi_ref, mine_ref, other_ref, out_ref):
    mine, other = mine_ref[...], other_ref[...]
    low = hi_ref[0] == 0
    first = jnp.where(low, mine, other)
    second = jnp.where(low, other, mine)
    for x in range(X):
        out_ref[x, :, :SHARD] = first
        out_ref[x, :, SHARD:] = second


def spread(z_hi, mine, other):
    return pl.pallas_call(
        spread_kernel,
        out_shape=jax.ShapeDtypeStruct((X, HALF_ROWS, Z_HI * SHARD), jnp.bfloat16),
        in_specs=[SMEM, VMEM, VMEM],
        out_specs=VMEM,
        compiler_params=pltpu.CompilerParams(vmem_limit_bytes=8 * 2**20),
        name="spread",
    )(z_hi.reshape(1), mine, other)


def stage_kernel(tok_hbm, tok_ref, sem):
    copy = pltpu.make_async_copy(tok_hbm.at[:, : X * SHARD], tok_ref, sem)
    copy.start()
    copy.wait()


def stage(tokens):
    return pl.pallas_call(
        stage_kernel,
        out_shape=pltpu.VMEM((tokens.shape[0], X * SHARD), tokens.dtype),
        in_specs=[HBM],
        out_specs=VMEM,
        scratch_shapes=[pltpu.SemaphoreType.DMA(())],
        compiler_params=pltpu.CompilerParams(vmem_limit_bytes=4 * 2**20),
        name="stage",
    )(in_hbm(tokens))


def product(w_ref, tok_ref, hi, first, pre):
    for x in range(X // 2):
        columns = pl.ds(pl.multiple_of((first + x) * SHARD, SHARD), SHARD)
        pre += lax.dot_general(
            w_ref[first + x, :, hi * SHARD : (hi + 1) * SHARD],
            tok_ref[:, columns],
            (((1,), (1,)), ((), ())),
            preferred_element_type=jnp.float32,
        )
    return pre


def own_kernel(w_ref, low_ref, tok_hbm, pre_ref, high_ref, sems):
    def copy(part):
        width = X // 2 * SHARD
        offset = pl.multiple_of(part * width, width)
        return pltpu.make_async_copy(
            tok_hbm.at[:, pl.ds(X * SHARD + offset, width)],
            high_ref.at[:, pl.ds(offset, width)],
            sems.at[part],
        )

    for part in range(2):
        copy(part).start()
    pre = jnp.zeros(pre_ref.shape, jnp.float32)
    for first in (0, X // 2):
        pre = product(w_ref, low_ref, 0, first, pre)

    def step(part, pre):
        copy(part).wait()
        return product(w_ref, high_ref, 1, part * (X // 2), pre)

    pre_ref[...] = lax.fori_loop(0, 2, step, pre)


def own_rows(weight, low, tokens):
    return pl.pallas_call(
        own_kernel,
        out_shape=[
            jax.ShapeDtypeStruct((HALF_ROWS, tokens.shape[0]), jnp.float32),
            pltpu.VMEM(low.shape, low.dtype),
        ],
        in_specs=[VMEM, VMEM, HBM],
        out_specs=[VMEM] * 2,
        scratch_shapes=[pltpu.SemaphoreType.DMA((2,))],
        compiler_params=pltpu.CompilerParams(vmem_limit_bytes=8 * 2**20),
        name="own_rows",
    )(weight, in_vmem(low), in_hbm(tokens))


def grad_half(delta, tok_ref, out_ref):
    for hi in range(Z_HI):
        for x in range(X):
            column = (hi * X + x) * PIECE
            out_ref[x, :, hi * PIECE : (hi + 1) * PIECE] = jnp.dot(
                delta, tok_ref[:, column : column + PIECE], preferred_element_type=jnp.float32
            ).astype(out_ref.dtype)


def give_kernel(core_ref, w_ref, pre_ref, cot_ref, low_ref, high_ref, delta_ref, out_ref):
    mine = pre_ref[...]
    theirs = jnp.zeros_like(mine)
    for hi, tok_ref in enumerate((low_ref, high_ref)):
        for x in (0, X // 2):
            theirs = product(w_ref, tok_ref, hi, x, theirs)
    first = core_ref[0] == 0
    pre = jnp.concatenate(
        [jnp.where(first, mine, theirs), jnp.where(first, theirs, mine)], axis=0
    )
    delta = (cot_ref[...].astype(jnp.float32) * slope(pre)).astype(jnp.bfloat16)
    delta_ref[...] = delta

    @pl.when(first)
    def _():
        grad_half(delta, high_ref, out_ref)

    @pl.when(jnp.logical_not(first))
    def _():
        grad_half(delta, low_ref, out_ref)


def give(core, weight, pre, cotangent, low, high):
    cotangent = cotangent.T
    return pl.pallas_call(
        give_kernel,
        out_shape=[
            jax.ShapeDtypeStruct(cotangent.shape, jnp.bfloat16),
            jax.ShapeDtypeStruct((X, ROWS, Z_HI * PIECE), jnp.bfloat16),
        ],
        in_specs=[SMEM] + [VMEM] * 5,
        out_specs=[VMEM] * 2,
        compiler_params=pltpu.CompilerParams(vmem_limit_bytes=8 * 2**20),
        name="give",
    )(core.reshape(1), weight, pre, cotangent, in_vmem(low), in_vmem(high))


def keep_kernel(core_ref, delta_ref, low_ref, high_ref, out_ref):
    first = core_ref[0] == 0
    delta = delta_ref[...]

    @pl.when(first)
    def _():
        grad_half(delta, low_ref, out_ref)

    @pl.when(jnp.logical_not(first))
    def _():
        grad_half(delta, high_ref, out_ref)


def keep(core, delta, low, high):
    return pl.pallas_call(
        keep_kernel,
        out_shape=jax.ShapeDtypeStruct((X, ROWS, Z_HI * PIECE), jnp.float32),
        in_specs=[SMEM] + [VMEM] * 3,
        out_specs=VMEM,
        compiler_params=pltpu.CompilerParams(vmem_limit_bytes=8 * 2**20),
        name="keep",
    )(core.reshape(1), delta, in_vmem(low), in_vmem(high))


def add_kernel(kept_ref, got_ref, out_ref):
    out_ref[...] = (kept_ref[...] + got_ref[...].astype(jnp.float32)).astype(jnp.bfloat16)


def add(kept, got):
    return pl.pallas_call(
        add_kernel,
        out_shape=jax.ShapeDtypeStruct(got.shape, jnp.bfloat16),
        in_specs=[VMEM] * 2,
        out_specs=VMEM,
        compiler_params=pltpu.CompilerParams(vmem_limit_bytes=8 * 2**20),
        name="add",
    )(kept, got)


def sum_kernel(in_ref, out_ref):
    total = jnp.sum(in_ref[...].astype(jnp.float32), axis=0)
    out_ref[...] = total.reshape(out_ref.shape).astype(jnp.bfloat16)


def sum_peers(parts):
    blocks = ROWS * Z_HI * PIECE_BLOCKS
    return pl.pallas_call(
        sum_kernel,
        out_shape=jax.ShapeDtypeStruct((blocks, BLOCK), jnp.bfloat16),
        in_specs=[VMEM],
        out_specs=VMEM,
        compiler_params=pltpu.CompilerParams(vmem_limit_bytes=8 * 2**20),
        name="sum_peers",
    )(parts)


def on_device(tokens, cotangent, w_codes, w_scales):
    core = lax.axis_index("core")
    z_hi = lax.axis_index("z_hi")

    mine = prepare(core, w_codes, w_scales)
    shift = [
        (lo * Z_HI + hi, (lo + Z_LO // 2) % Z_LO * Z_HI + (1 - hi))
        for lo in range(Z_LO)
        for hi in range(Z_HI)
    ]
    other = lax.ppermute(mine, ("z_lo", "z_hi"), shift)
    late_tokens, _ = lax.optimization_barrier((tokens, mine))
    low = stage(late_tokens)
    copies = spread(z_hi, mine, other)
    copies, low = lax.optimization_barrier((copies, low))
    half = lax.all_to_all(copies, "x", split_axis=0, concat_axis=0, tiled=True)

    theirs = lax.ppermute(half, "core", SWAP)
    pre, high = own_rows(half, low, tokens)

    delta, given = give(core, theirs, pre, cotangent, low, high)
    got = lax.ppermute(given, "core", SWAP)
    kept = keep(core, delta, low, high)

    from_x = lax.all_to_all(add(kept, got), "x", split_axis=0, concat_axis=0, tiled=True)
    by_yz = sum_peers(from_x).reshape(Z_LO * Y * Z_HI, PIECE_BLOCKS, BLOCK)
    from_yz = lax.all_to_all(
        by_yz, ("z_lo", "y", "z_hi"), split_axis=0, concat_axis=0, tiled=True
    )
    return jnp.sum(from_yz.astype(jnp.float32), axis=0)


def solution(mesh):
    fine = Mesh(
        mesh.devices.reshape(Z_LO, Y, CORE, Z_HI, X), ("z_lo", "y", "core", "z_hi", "x")
    )
    outer, inner = ("z_lo", "y", "core"), ("z_hi", "x")
    in_specs = (
        P(outer + inner, None),
        P(outer + inner, None),
        P(None, inner, None),
        P(None, inner),
    )
    return jax.shard_map(
        on_device, mesh=fine, in_specs=in_specs, out_specs=P(outer + inner, None), check_vma=False
    )
```

```python
import functools

import jax
import jax.numpy as jnp
from jax import lax
from jax.experimental import pallas as pl
from jax.experimental.pallas import tpu as pltpu
from jax.sharding import Mesh, PartitionSpec as P

BLOCK = 128
Z_LO, Y, CORE, Z_HI, X = 6, 8, 2, 2, 4
ROWS = 48
HALF_ROWS = ROWS // CORE
STAGED = 5120
SHARD = 1024
PIECE = 512
PIECE_BLOCKS = PIECE // BLOCK
VMEM = pl.BlockSpec(memory_space=pltpu.VMEM)
HBM = pl.BlockSpec(memory_space=pltpu.HBM)
SMEM = pl.BlockSpec(memory_space=pltpu.SMEM)
SWAP = ((0, 1), (1, 0))


def in_vmem(array):
    return pltpu.with_memory_space_constraint(array, pltpu.VMEM)


def in_hbm(array):
    return pltpu.with_memory_space_constraint(array, pltpu.HBM)


def slope(pre):
    sig = jax.nn.sigmoid(pre)
    return sig * (1.0 + pre * (1.0 - sig))


def prepare_kernel(core_ref, codes_hbm, scales_hbm, mine_ref, codes_ref, scales_ref, sems):
    copies = [
        pltpu.make_async_copy(
            codes_hbm.at[pl.ds(core_ref[0] * HALF_ROWS, HALF_ROWS)], codes_ref, sems.at[0]
        ),
        pltpu.make_async_copy(scales_hbm, scales_ref, sems.at[1]),
    ]
    for copy in copies:
        copy.start()
    for copy in copies:
        copy.wait()
    codes = codes_ref[...].astype(jnp.float32).reshape(HALF_ROWS, SHARD)
    scales = scales_ref[...].T
    scales = jnp.where(core_ref[0] == 0, scales[:HALF_ROWS], scales[HALF_ROWS:])
    for k in range(SHARD // BLOCK):
        block = slice(k * BLOCK, (k + 1) * BLOCK)
        mine_ref[:, block] = (codes[:, block] * scales[:, k : k + 1]).astype(jnp.bfloat16)


def prepare(core, w_codes, w_scales):
    scales = w_scales.T
    return pl.pallas_call(
        prepare_kernel,
        out_shape=jax.ShapeDtypeStruct((HALF_ROWS, SHARD), jnp.bfloat16),
        in_specs=[SMEM, HBM, HBM],
        out_specs=VMEM,
        scratch_shapes=[
            pltpu.VMEM((HALF_ROWS,) + w_codes.shape[1:], w_codes.dtype),
            pltpu.VMEM(scales.shape, scales.dtype),
            pltpu.SemaphoreType.DMA((2,)),
        ],
        compiler_params=pltpu.CompilerParams(vmem_limit_bytes=8 * 2**20),
        name="prepare",
    )(core.reshape(1), in_hbm(w_codes), in_hbm(scales))


def spread_kernel(hi_ref, mine_ref, other_ref, out_ref):
    mine, other = mine_ref[...], other_ref[...]
    low = hi_ref[0] == 0
    first = jnp.where(low, mine, other)
    second = jnp.where(low, other, mine)
    for x in range(X):
        out_ref[x, :, :SHARD] = first
        out_ref[x, :, SHARD:] = second


def spread(z_hi, mine, other):
    return pl.pallas_call(
        spread_kernel,
        out_shape=jax.ShapeDtypeStruct((X, HALF_ROWS, Z_HI * SHARD), jnp.bfloat16),
        in_specs=[SMEM, VMEM, VMEM],
        out_specs=VMEM,
        compiler_params=pltpu.CompilerParams(vmem_limit_bytes=8 * 2**20),
        name="spread",
    )(z_hi.reshape(1), mine, other)


def stage_kernel(tok_hbm, tok_ref, sem, *, first):
    width = tok_ref.shape[1]
    copy = pltpu.make_async_copy(tok_hbm.at[:, first : first + width], tok_ref, sem)
    copy.start()
    copy.wait()


def stage(tokens, first, width):
    return pl.pallas_call(
        functools.partial(stage_kernel, first=first),
        out_shape=pltpu.VMEM((tokens.shape[0], width), tokens.dtype),
        in_specs=[HBM],
        out_specs=VMEM,
        scratch_shapes=[pltpu.SemaphoreType.DMA(())],
        compiler_params=pltpu.CompilerParams(vmem_limit_bytes=4 * 2**20),
        name="stage",
    )(in_hbm(tokens))


def columns_of(low_ref, high_ref, first, width):
    if first < low_ref.shape[1]:
        return low_ref[:, first : first + width]
    first -= low_ref.shape[1]
    return high_ref[:, first : first + width]


def grad_half(delta, low_ref, high_ref, core, out_ref):
    for hi in range(Z_HI):
        for x in range(X):
            column = ((core * Z_HI + hi) * X + x) * PIECE
            out_ref[x, :, hi * PIECE : (hi + 1) * PIECE] = jnp.dot(
                delta,
                columns_of(low_ref, high_ref, column, PIECE),
                preferred_element_type=jnp.float32,
            ).astype(out_ref.dtype)


def give_kernel(core_ref, mine_ref, theirs_ref, cot_ref, low_ref, high_ref, delta_ref, out_ref):
    pre = jnp.zeros((ROWS, cot_ref.shape[1]), jnp.float32)
    for hi in range(Z_HI):
        for x in range(X):
            part = slice(hi * SHARD, (hi + 1) * SHARD)
            rows = jnp.concatenate([mine_ref[x, :, part], theirs_ref[x, :, part]], axis=0)
            pre += lax.dot_general(
                rows,
                columns_of(low_ref, high_ref, (hi * X + x) * SHARD, SHARD),
                (((1,), (1,)), ((), ())),
                preferred_element_type=jnp.float32,
            )
    mine, theirs = pre[:HALF_ROWS], pre[HALF_ROWS:]
    first = core_ref[0] == 0
    pre = jnp.concatenate(
        [jnp.where(first, mine, theirs), jnp.where(first, theirs, mine)], axis=0
    )
    delta = (cot_ref[...].astype(jnp.float32) * slope(pre)).astype(jnp.bfloat16)
    delta_ref[...] = delta

    @pl.when(first)
    def _():
        grad_half(delta, low_ref, high_ref, 1, out_ref)

    @pl.when(jnp.logical_not(first))
    def _():
        grad_half(delta, low_ref, high_ref, 0, out_ref)


def give(core, mine, theirs, cotangent, low, high):
    cotangent = cotangent.T
    return pl.pallas_call(
        give_kernel,
        out_shape=[
            jax.ShapeDtypeStruct(cotangent.shape, jnp.bfloat16),
            jax.ShapeDtypeStruct((X, ROWS, Z_HI * PIECE), jnp.bfloat16),
        ],
        in_specs=[SMEM] + [VMEM] * 5,
        out_specs=[VMEM] * 2,
        compiler_params=pltpu.CompilerParams(vmem_limit_bytes=8 * 2**20),
        name="give",
    )(core.reshape(1), mine, theirs, cotangent, in_vmem(low), in_vmem(high))


def keep_kernel(core_ref, delta_ref, low_ref, high_ref, out_ref):
    first = core_ref[0] == 0
    delta = delta_ref[...]

    @pl.when(first)
    def _():
        grad_half(delta, low_ref, high_ref, 0, out_ref)

    @pl.when(jnp.logical_not(first))
    def _():
        grad_half(delta, low_ref, high_ref, 1, out_ref)


def keep(core, delta, low, high):
    return pl.pallas_call(
        keep_kernel,
        out_shape=jax.ShapeDtypeStruct((X, ROWS, Z_HI * PIECE), jnp.float32),
        in_specs=[SMEM] + [VMEM] * 3,
        out_specs=VMEM,
        compiler_params=pltpu.CompilerParams(vmem_limit_bytes=8 * 2**20),
        name="keep",
    )(core.reshape(1), delta, in_vmem(low), in_vmem(high))


def add_kernel(kept_ref, got_ref, out_ref):
    out_ref[...] = (kept_ref[...] + got_ref[...].astype(jnp.float32)).astype(jnp.bfloat16)


def add(kept, got):
    return pl.pallas_call(
        add_kernel,
        out_shape=jax.ShapeDtypeStruct(got.shape, jnp.bfloat16),
        in_specs=[VMEM] * 2,
        out_specs=VMEM,
        compiler_params=pltpu.CompilerParams(vmem_limit_bytes=8 * 2**20),
        name="add",
    )(kept, got)


def sum_kernel(in_ref, out_ref):
    total = jnp.sum(in_ref[...].astype(jnp.float32), axis=0)
    out_ref[...] = total.reshape(out_ref.shape).astype(jnp.bfloat16)


def sum_peers(parts):
    blocks = ROWS * Z_HI * PIECE_BLOCKS
    return pl.pallas_call(
        sum_kernel,
        out_shape=jax.ShapeDtypeStruct((blocks, BLOCK), jnp.bfloat16),
        in_specs=[VMEM],
        out_specs=VMEM,
        compiler_params=pltpu.CompilerParams(vmem_limit_bytes=8 * 2**20),
        name="sum_peers",
    )(parts)


def final_kernel(in_ref, out_ref):
    pairs = in_ref[...].astype(jnp.float32).reshape(-1, 2 * PIECE_BLOCKS, BLOCK)
    pair = jnp.sum(pairs, axis=0)
    out_ref[...] = pair[:PIECE_BLOCKS] + pair[PIECE_BLOCKS:]


def final_sum(parts):
    return pl.pallas_call(
        final_kernel,
        out_shape=jax.ShapeDtypeStruct(parts.shape[1:], jnp.float32),
        in_specs=[VMEM],
        out_specs=VMEM,
        compiler_params=pltpu.CompilerParams(vmem_limit_bytes=8 * 2**20),
        name="final_sum",
    )(parts.reshape(-1, BLOCK))


def on_device(tokens, cotangent, w_codes, w_scales):
    core = lax.axis_index("core")
    z_hi = lax.axis_index("z_hi")

    mine = prepare(core, w_codes, w_scales)
    shift = [
        (lo * Z_HI + hi, (lo + Z_LO // 2) % Z_LO * Z_HI + (1 - hi))
        for lo in range(Z_LO)
        for hi in range(Z_HI)
    ]
    other = lax.ppermute(mine, ("z_lo", "z_hi"), shift)
    late_tokens, _ = lax.optimization_barrier((tokens, mine))
    low = stage(late_tokens, 0, STAGED)
    copies = spread(z_hi, mine, other)
    copies, low = lax.optimization_barrier((copies, low))
    half = lax.all_to_all(copies, "x", split_axis=0, concat_axis=0, tiled=True)

    theirs = lax.ppermute(half, "core", SWAP)
    late_tokens, _ = lax.optimization_barrier((tokens, half))
    high = stage(late_tokens, STAGED, tokens.shape[1] - STAGED)

    delta, given = give(core, half, theirs, cotangent, low, high)
    got = lax.ppermute(given, "core", SWAP)
    kept = keep(core, delta, low, high)

    from_x = lax.all_to_all(add(kept, got), "x", split_axis=0, concat_axis=0, tiled=True)
    by_yz = sum_peers(from_x).reshape(Z_LO * Y * Z_HI, PIECE_BLOCKS, BLOCK)
    from_yz = lax.all_to_all(
        by_yz, ("z_lo", "y", "z_hi"), split_axis=0, concat_axis=0, tiled=True
    )
    return final_sum(from_yz)


def solution(mesh):
    fine = Mesh(
        mesh.devices.reshape(Z_LO, Y, CORE, Z_HI, X), ("z_lo", "y", "core", "z_hi", "x")
    )
    outer, inner = ("z_lo", "y", "core"), ("z_hi", "x")
    in_specs = (
        P(outer + inner, None),
        P(outer + inner, None),
        P(None, inner, None),
        P(None, inner),
    )
    return jax.shard_map(
        on_device, mesh=fine, in_specs=in_specs, out_specs=P(outer + inner, None), check_vma=False
    )
```

```python
import functools

import jax
import jax.numpy as jnp
from jax import lax
from jax.experimental import pallas as pl
from jax.experimental.pallas import tpu as pltpu
from jax.sharding import Mesh, PartitionSpec as P

BLOCK = 128
Z_LO, Y_HI, Y_LO, CORE, Z_HI, X = 6, 4, 2, 2, 2, 4
ROWS = 48
HALF_ROWS = ROWS // CORE
STAGED = 5120
SHARD = 1024
PIECE = 512
PIECE_BLOCKS = PIECE // BLOCK
VMEM = pl.BlockSpec(memory_space=pltpu.VMEM)
HBM = pl.BlockSpec(memory_space=pltpu.HBM)
SMEM = pl.BlockSpec(memory_space=pltpu.SMEM)
SWAP = ((0, 1), (1, 0))


def in_vmem(array):
    return pltpu.with_memory_space_constraint(array, pltpu.VMEM)


def in_hbm(array):
    return pltpu.with_memory_space_constraint(array, pltpu.HBM)


def slope(pre):
    sig = jax.nn.sigmoid(pre)
    return sig * (1.0 + pre * (1.0 - sig))


def prepare_kernel(core_ref, codes_hbm, scales_hbm, mine_ref, codes_ref, scales_ref, turned_ref, sems):
    copies = [
        pltpu.make_async_copy(
            codes_hbm.at[:, core_ref[0]], codes_ref, sems.at[0]
        ),
        pltpu.make_async_copy(scales_hbm, scales_ref, sems.at[1]),
    ]
    for copy in copies:
        copy.start()
    for copy in copies:
        copy.wait()
    codes = codes_ref[...].astype(jnp.float32).reshape(HALF_ROWS, SHARD)
    count = SHARD // BLOCK
    turned_ref[:, :count] = scales_ref[...].T
    even, odd = (turned_ref[pl.ds(y, HALF_ROWS, stride=Y_LO), :] for y in range(Y_LO))
    scales = jnp.where(core_ref[0] == 0, even, odd)
    for k in range(count):
        block = slice(k * BLOCK, (k + 1) * BLOCK)
        mine_ref[:, block] = (codes[:, block] * scales[:, k : k + 1]).astype(jnp.bfloat16)


def prepare(core, w_codes, w_scales):
    w_codes = w_codes.reshape((HALF_ROWS, Y_LO) + w_codes.shape[1:])
    scales = w_scales.T
    return pl.pallas_call(
        prepare_kernel,
        out_shape=jax.ShapeDtypeStruct((HALF_ROWS, SHARD), jnp.bfloat16),
        in_specs=[SMEM, HBM, HBM],
        out_specs=VMEM,
        scratch_shapes=[
            pltpu.VMEM((HALF_ROWS,) + w_codes.shape[2:], w_codes.dtype),
            pltpu.VMEM(scales.shape, scales.dtype),
            pltpu.VMEM((ROWS, BLOCK), scales.dtype),
            pltpu.SemaphoreType.DMA((2,)),
        ],
        compiler_params=pltpu.CompilerParams(vmem_limit_bytes=8 * 2**20),
        name="prepare",
    )(core.reshape(1), in_hbm(w_codes), in_hbm(scales))


def spread_kernel(hi_ref, mine_ref, other_ref, out_ref):
    mine, other = mine_ref[...], other_ref[...]
    low = hi_ref[0] == 0
    first = jnp.where(low, mine, other)
    second = jnp.where(low, other, mine)
    for x in range(X):
        out_ref[x, :, :SHARD] = first
        out_ref[x, :, SHARD:] = second


def spread(z_hi, mine, other):
    return pl.pallas_call(
        spread_kernel,
        out_shape=jax.ShapeDtypeStruct((X, HALF_ROWS, Z_HI * SHARD), jnp.bfloat16),
        in_specs=[SMEM, VMEM, VMEM],
        out_specs=VMEM,
        compiler_params=pltpu.CompilerParams(vmem_limit_bytes=8 * 2**20),
        name="spread",
    )(z_hi.reshape(1), mine, other)


def stage_kernel(tok_hbm, tok_ref, sem, *, first):
    width = tok_ref.shape[1]
    copy = pltpu.make_async_copy(tok_hbm.at[:, first : first + width], tok_ref, sem)
    copy.start()
    copy.wait()


def stage(tokens, first, width):
    return pl.pallas_call(
        functools.partial(stage_kernel, first=first),
        out_shape=pltpu.VMEM((tokens.shape[0], width), tokens.dtype),
        in_specs=[HBM],
        out_specs=VMEM,
        scratch_shapes=[pltpu.SemaphoreType.DMA(())],
        compiler_params=pltpu.CompilerParams(vmem_limit_bytes=4 * 2**20),
        name="stage",
    )(in_hbm(tokens))


def columns_of(low_ref, high_ref, first, width):
    if first < low_ref.shape[1]:
        return low_ref[:, first : first + width]
    first -= low_ref.shape[1]
    return high_ref[:, first : first + width]


def grad_half(delta, low_ref, high_ref, core, out_ref):
    for hi in range(Z_HI):
        for x in range(X):
            column = ((core * Z_HI + hi) * X + x) * PIECE
            grad = jnp.dot(
                delta,
                columns_of(low_ref, high_ref, column, PIECE),
                preferred_element_type=jnp.float32,
            )
            for y in range(Y_LO):
                out_ref[y * X + x, :, hi * PIECE : (hi + 1) * PIECE] = grad[
                    y * HALF_ROWS : (y + 1) * HALF_ROWS
                ].astype(out_ref.dtype)


def give_kernel(core_ref, mine_ref, theirs_ref, cot_ref, low_ref, high_ref, delta_ref, out_ref):
    pre = jnp.zeros((ROWS, cot_ref.shape[1]), jnp.float32)
    for hi in range(Z_HI):
        for x in range(X):
            part = slice(hi * SHARD, (hi + 1) * SHARD)
            rows = jnp.concatenate([mine_ref[x, :, part], theirs_ref[x, :, part]], axis=0)
            pre += lax.dot_general(
                rows,
                columns_of(low_ref, high_ref, (hi * X + x) * SHARD, SHARD),
                (((1,), (1,)), ((), ())),
                preferred_element_type=jnp.float32,
            )
    mine, theirs = pre[:HALF_ROWS], pre[HALF_ROWS:]
    first = core_ref[0] == 0
    pre = jnp.concatenate(
        [jnp.where(first, mine, theirs), jnp.where(first, theirs, mine)], axis=0
    )
    delta = (cot_ref[...].astype(jnp.float32) * slope(pre)).astype(jnp.bfloat16)
    delta_ref[...] = delta

    @pl.when(first)
    def _():
        grad_half(delta, low_ref, high_ref, 1, out_ref)

    @pl.when(jnp.logical_not(first))
    def _():
        grad_half(delta, low_ref, high_ref, 0, out_ref)


def give(core, mine, theirs, cotangent, low, high):
    return pl.pallas_call(
        give_kernel,
        out_shape=[
            jax.ShapeDtypeStruct(cotangent.shape, jnp.bfloat16),
            jax.ShapeDtypeStruct((Y_LO * X, HALF_ROWS, Z_HI * PIECE), jnp.bfloat16),
        ],
        in_specs=[SMEM] + [VMEM] * 5,
        out_specs=[VMEM] * 2,
        compiler_params=pltpu.CompilerParams(vmem_limit_bytes=8 * 2**20),
        name="give",
    )(core.reshape(1), mine, theirs, cotangent, in_vmem(low), in_vmem(high))


def keep_kernel(core_ref, delta_ref, low_ref, high_ref, out_ref):
    first = core_ref[0] == 0
    delta = delta_ref[...]

    @pl.when(first)
    def _():
        grad_half(delta, low_ref, high_ref, 0, out_ref)

    @pl.when(jnp.logical_not(first))
    def _():
        grad_half(delta, low_ref, high_ref, 1, out_ref)


def keep(core, delta, low, high):
    return pl.pallas_call(
        keep_kernel,
        out_shape=jax.ShapeDtypeStruct((Y_LO * X, HALF_ROWS, Z_HI * PIECE), jnp.float32),
        in_specs=[SMEM] + [VMEM] * 3,
        out_specs=VMEM,
        compiler_params=pltpu.CompilerParams(vmem_limit_bytes=8 * 2**20),
        name="keep",
    )(core.reshape(1), delta, in_vmem(low), in_vmem(high))


def add_kernel(kept_ref, got_ref, out_ref):
    out_ref[...] = (kept_ref[...] + got_ref[...].astype(jnp.float32)).astype(jnp.bfloat16)


def add(kept, got):
    return pl.pallas_call(
        add_kernel,
        out_shape=jax.ShapeDtypeStruct(got.shape, jnp.bfloat16),
        in_specs=[VMEM] * 2,
        out_specs=VMEM,
        compiler_params=pltpu.CompilerParams(vmem_limit_bytes=8 * 2**20),
        name="add",
    )(kept, got)


def sum_kernel(in_ref, out_ref):
    total = jnp.sum(in_ref[...].astype(jnp.float32), axis=0)
    out_ref[...] = total.reshape(out_ref.shape).astype(jnp.bfloat16)


def sum_peers(parts):
    blocks = HALF_ROWS * Z_HI * PIECE_BLOCKS
    return pl.pallas_call(
        sum_kernel,
        out_shape=jax.ShapeDtypeStruct((blocks, BLOCK), jnp.bfloat16),
        in_specs=[VMEM],
        out_specs=VMEM,
        compiler_params=pltpu.CompilerParams(vmem_limit_bytes=8 * 2**20),
        name="sum_peers",
    )(parts)


def final_kernel(in_ref, out_ref):
    pairs = in_ref[...].astype(jnp.float32).reshape(-1, 2 * PIECE_BLOCKS, BLOCK)
    pair = jnp.sum(pairs, axis=0)
    out_ref[...] = pair[:PIECE_BLOCKS] + pair[PIECE_BLOCKS:]


def final_sum(parts):
    return pl.pallas_call(
        final_kernel,
        out_shape=jax.ShapeDtypeStruct(parts.shape[1:], jnp.float32),
        in_specs=[VMEM],
        out_specs=VMEM,
        compiler_params=pltpu.CompilerParams(vmem_limit_bytes=8 * 2**20),
        name="final_sum",
    )(parts.reshape(-1, BLOCK))


def on_device(tokens, cotangent, w_codes, w_scales):
    core = lax.axis_index("core")
    z_hi = lax.axis_index("z_hi")

    mine = prepare(core, w_codes, w_scales)
    shift = [
        (lo * Z_HI + hi, (lo + Z_LO // 2) % Z_LO * Z_HI + (1 - hi))
        for lo in range(Z_LO)
        for hi in range(Z_HI)
    ]
    other = lax.ppermute(mine, ("z_lo", "z_hi"), shift)
    late_tokens, cotangent, _ = lax.optimization_barrier((tokens, cotangent, mine))
    low = stage(late_tokens, 0, STAGED)
    cot = cotangent.T.reshape(HALF_ROWS, Y_LO, -1).transpose(1, 0, 2).reshape(ROWS, -1)
    copies = spread(z_hi, mine, other)
    copies, low, cot = lax.optimization_barrier((copies, low, cot))
    half = lax.all_to_all(copies, "x", split_axis=0, concat_axis=0, tiled=True)

    theirs = lax.ppermute(half, "core", SWAP)
    late_tokens, _ = lax.optimization_barrier((tokens, half))
    high = stage(late_tokens, STAGED, tokens.shape[1] - STAGED)

    delta, given = give(core, half, theirs, cot, low, high)
    got = lax.ppermute(given, "core", SWAP)
    kept = keep(core, delta, low, high)

    from_x = lax.all_to_all(
        add(kept, got), ("y_lo", "x"), split_axis=0, concat_axis=0, tiled=True
    )
    by_yz = sum_peers(from_x).reshape(Z_LO * Y_HI * Z_HI, PIECE_BLOCKS, BLOCK)
    from_yz = lax.all_to_all(
        by_yz, ("z_lo", "y_hi", "z_hi"), split_axis=0, concat_axis=0, tiled=True
    )
    return final_sum(from_yz)


def solution(mesh):
    fine = Mesh(
        mesh.devices.reshape(Z_LO, Y_HI, Y_LO, CORE, Z_HI, X),
        ("z_lo", "y_hi", "y_lo", "core", "z_hi", "x"),
    )
    outer, inner = ("z_lo", "y_hi", "y_lo", "core"), ("z_hi", "x")
    in_specs = (
        P(outer + inner, None),
        P(outer + inner, None),
        P(None, inner, None),
        P(None, inner),
    )
    return jax.shard_map(
        on_device, mesh=fine, in_specs=in_specs, out_specs=P(outer + inner, None), check_vma=False
    )
```

```python
import functools

import jax
import jax.numpy as jnp
from jax import lax
from jax.experimental import pallas as pl
from jax.experimental.pallas import tpu as pltpu
from jax.sharding import Mesh, PartitionSpec as P

BLOCK = 128
Z_LO, Y_HI, Y_LO, CORE, Z_HI, X = 6, 4, 2, 2, 2, 4
ROWS = 48
HALF_ROWS = ROWS // CORE
STAGED = 5120
SHARD = 1024
PIECE = 512
PIECE_BLOCKS = PIECE // BLOCK
VMEM = pl.BlockSpec(memory_space=pltpu.VMEM)
HBM = pl.BlockSpec(memory_space=pltpu.HBM)
SMEM = pl.BlockSpec(memory_space=pltpu.SMEM)
SWAP = ((0, 1), (1, 0))


def in_vmem(array):
    return pltpu.with_memory_space_constraint(array, pltpu.VMEM)


def in_hbm(array):
    return pltpu.with_memory_space_constraint(array, pltpu.HBM)


def slope(pre):
    sig = jax.nn.sigmoid(pre)
    return sig * (1.0 + pre * (1.0 - sig))


def prepare_kernel(place_ref, codes_hbm, scales_hbm, mine_ref, codes_ref, scales_ref, turned_ref, sems):
    core, y_lo = lax.rem(place_ref[0], CORE), lax.div(place_ref[0], CORE)
    copies = [
        pltpu.make_async_copy(codes_hbm.at[:, core], codes_ref, sems.at[0]),
        pltpu.make_async_copy(scales_hbm, scales_ref, sems.at[1]),
    ]
    for copy in copies:
        copy.start()
    for copy in copies:
        copy.wait()
    codes = codes_ref[...].astype(jnp.float32).reshape(HALF_ROWS, SHARD)
    count = SHARD // BLOCK
    turned_ref[:, :count] = scales_ref[...].T
    even, odd = (turned_ref[pl.ds(y, HALF_ROWS, stride=Y_LO), :] for y in range(Y_LO))
    scales = jnp.where(core == 0, even, odd)
    parts = [codes[:, k * BLOCK : (k + 1) * BLOCK] * scales[:, k : k + 1] for k in range(count)]
    for k in range(count // Y_LO):
        part = jnp.where(y_lo == 0, parts[k], parts[count // Y_LO + k])
        mine_ref[:, k * BLOCK : (k + 1) * BLOCK] = part.astype(jnp.bfloat16)


def prepare(place, w_codes, w_scales):
    w_codes = w_codes.reshape((HALF_ROWS, Y_LO) + w_codes.shape[1:])
    scales = w_scales.T
    return pl.pallas_call(
        prepare_kernel,
        out_shape=jax.ShapeDtypeStruct((HALF_ROWS, PIECE), jnp.bfloat16),
        in_specs=[SMEM, HBM, HBM],
        out_specs=VMEM,
        scratch_shapes=[
            pltpu.VMEM((HALF_ROWS,) + w_codes.shape[2:], w_codes.dtype),
            pltpu.VMEM(scales.shape, scales.dtype),
            pltpu.VMEM((ROWS, BLOCK), scales.dtype),
            pltpu.SemaphoreType.DMA((2,)),
        ],
        compiler_params=pltpu.CompilerParams(vmem_limit_bytes=8 * 2**20),
        name="prepare",
    )(place.reshape(1), in_hbm(w_codes), in_hbm(scales))


def spread_kernel(hi_ref, mine_ref, other_ref, out_ref):
    mine, other = mine_ref[...], other_ref[...]
    low = hi_ref[0] == 0
    first = jnp.where(low, mine, other)
    second = jnp.where(low, other, mine)
    for peer in range(Y_LO * X):
        out_ref[peer, :, :PIECE] = first
        out_ref[peer, :, PIECE:] = second


def spread(z_hi, mine, other):
    return pl.pallas_call(
        spread_kernel,
        out_shape=jax.ShapeDtypeStruct((Y_LO * X, HALF_ROWS, Z_HI * PIECE), jnp.bfloat16),
        in_specs=[SMEM, VMEM, VMEM],
        out_specs=VMEM,
        compiler_params=pltpu.CompilerParams(vmem_limit_bytes=8 * 2**20),
        name="spread",
    )(z_hi.reshape(1), mine, other)


def stage_kernel(tok_hbm, tok_ref, sem, *, first):
    width = tok_ref.shape[1]
    copy = pltpu.make_async_copy(tok_hbm.at[:, first : first + width], tok_ref, sem)
    copy.start()
    copy.wait()


def stage(tokens, first, width):
    return pl.pallas_call(
        functools.partial(stage_kernel, first=first),
        out_shape=pltpu.VMEM((tokens.shape[0], width), tokens.dtype),
        in_specs=[HBM],
        out_specs=VMEM,
        scratch_shapes=[pltpu.SemaphoreType.DMA(())],
        compiler_params=pltpu.CompilerParams(vmem_limit_bytes=4 * 2**20),
        name="stage",
    )(in_hbm(tokens))


def columns_of(low_ref, high_ref, first, width):
    if first < low_ref.shape[1]:
        return low_ref[:, first : first + width]
    first -= low_ref.shape[1]
    return high_ref[:, first : first + width]


def grad_half(delta, low_ref, high_ref, core, out_ref):
    for hi in range(Z_HI):
        for x in range(X):
            column = ((core * Z_HI + hi) * X + x) * PIECE
            grad = jnp.dot(
                delta,
                columns_of(low_ref, high_ref, column, PIECE),
                preferred_element_type=jnp.float32,
            )
            for y in range(Y_LO):
                out_ref[y * X + x, :, hi * PIECE : (hi + 1) * PIECE] = grad[
                    y * HALF_ROWS : (y + 1) * HALF_ROWS
                ].astype(out_ref.dtype)


def give_kernel(core_ref, mine_ref, theirs_ref, cot_ref, low_ref, high_ref, delta_ref, out_ref):
    pre = jnp.zeros((ROWS, cot_ref.shape[1]), jnp.float32)
    for hi in range(Z_HI):
        for x in range(X):
            part = slice(hi * PIECE, (hi + 1) * PIECE)
            rows = [
                jnp.concatenate([ref[y * X + x, :, part] for y in range(Y_LO)], axis=1)
                for ref in (mine_ref, theirs_ref)
            ]
            rows = jnp.concatenate(rows, axis=0)
            pre += lax.dot_general(
                rows,
                columns_of(low_ref, high_ref, (hi * X + x) * SHARD, SHARD),
                (((1,), (1,)), ((), ())),
                preferred_element_type=jnp.float32,
            )
    mine, theirs = pre[:HALF_ROWS], pre[HALF_ROWS:]
    first = core_ref[0] == 0
    pre = jnp.concatenate(
        [jnp.where(first, mine, theirs), jnp.where(first, theirs, mine)], axis=0
    )
    delta = (cot_ref[...].astype(jnp.float32) * slope(pre)).astype(jnp.bfloat16)
    delta_ref[...] = delta

    @pl.when(first)
    def _():
        grad_half(delta, low_ref, high_ref, 1, out_ref)

    @pl.when(jnp.logical_not(first))
    def _():
        grad_half(delta, low_ref, high_ref, 0, out_ref)


def give(core, mine, theirs, cotangent, low, high):
    return pl.pallas_call(
        give_kernel,
        out_shape=[
            jax.ShapeDtypeStruct(cotangent.shape, jnp.bfloat16),
            jax.ShapeDtypeStruct((Y_LO * X, HALF_ROWS, Z_HI * PIECE), jnp.bfloat16),
        ],
        in_specs=[SMEM] + [VMEM] * 5,
        out_specs=[VMEM] * 2,
        compiler_params=pltpu.CompilerParams(vmem_limit_bytes=8 * 2**20),
        name="give",
    )(core.reshape(1), mine, theirs, cotangent, in_vmem(low), in_vmem(high))


def keep_kernel(core_ref, delta_ref, low_ref, high_ref, out_ref):
    first = core_ref[0] == 0
    delta = delta_ref[...]

    @pl.when(first)
    def _():
        grad_half(delta, low_ref, high_ref, 0, out_ref)

    @pl.when(jnp.logical_not(first))
    def _():
        grad_half(delta, low_ref, high_ref, 1, out_ref)


def keep(core, delta, low, high):
    return pl.pallas_call(
        keep_kernel,
        out_shape=jax.ShapeDtypeStruct((Y_LO * X, HALF_ROWS, Z_HI * PIECE), jnp.float32),
        in_specs=[SMEM] + [VMEM] * 3,
        out_specs=VMEM,
        compiler_params=pltpu.CompilerParams(vmem_limit_bytes=8 * 2**20),
        name="keep",
    )(core.reshape(1), delta, in_vmem(low), in_vmem(high))


def add_kernel(kept_ref, got_ref, out_ref):
    out_ref[...] = (kept_ref[...] + got_ref[...].astype(jnp.float32)).astype(jnp.bfloat16)


def add(kept, got):
    return pl.pallas_call(
        add_kernel,
        out_shape=jax.ShapeDtypeStruct(got.shape, jnp.bfloat16),
        in_specs=[VMEM] * 2,
        out_specs=VMEM,
        compiler_params=pltpu.CompilerParams(vmem_limit_bytes=8 * 2**20),
        name="add",
    )(kept, got)


def sum_kernel(in_ref, out_ref):
    total = jnp.sum(in_ref[...].astype(jnp.float32), axis=0)
    out_ref[...] = total.reshape(out_ref.shape).astype(jnp.bfloat16)


def sum_peers(parts):
    blocks = HALF_ROWS * Z_HI * PIECE_BLOCKS
    return pl.pallas_call(
        sum_kernel,
        out_shape=jax.ShapeDtypeStruct((blocks, BLOCK), jnp.bfloat16),
        in_specs=[VMEM],
        out_specs=VMEM,
        compiler_params=pltpu.CompilerParams(vmem_limit_bytes=8 * 2**20),
        name="sum_peers",
    )(parts)


def final_kernel(in_ref, out_ref):
    pairs = in_ref[...].astype(jnp.float32).reshape(-1, 2 * PIECE_BLOCKS, BLOCK)
    pair = jnp.sum(pairs, axis=0)
    out_ref[...] = pair[:PIECE_BLOCKS] + pair[PIECE_BLOCKS:]


def final_sum(parts):
    return pl.pallas_call(
        final_kernel,
        out_shape=jax.ShapeDtypeStruct(parts.shape[1:], jnp.float32),
        in_specs=[VMEM],
        out_specs=VMEM,
        compiler_params=pltpu.CompilerParams(vmem_limit_bytes=8 * 2**20),
        name="final_sum",
    )(parts.reshape(-1, BLOCK))


def on_device(tokens, cotangent, w_codes, w_scales):
    core = lax.axis_index("core")
    z_hi = lax.axis_index("z_hi")

    mine = prepare(core + CORE * lax.axis_index("y_lo"), w_codes, w_scales)
    shift = [
        (lo * Z_HI + hi, (lo + Z_LO // 2) % Z_LO * Z_HI + (1 - hi))
        for lo in range(Z_LO)
        for hi in range(Z_HI)
    ]
    other = lax.ppermute(mine, ("z_lo", "z_hi"), shift)
    late_tokens, cotangent, _ = lax.optimization_barrier((tokens, cotangent, mine))
    low = stage(late_tokens, 0, STAGED)
    cot = cotangent.T.reshape(HALF_ROWS, Y_LO, -1).transpose(1, 0, 2).reshape(ROWS, -1)
    copies = spread(z_hi, mine, other)
    copies, low, cot = lax.optimization_barrier((copies, low, cot))
    half = lax.all_to_all(copies, ("y_lo", "x"), split_axis=0, concat_axis=0, tiled=True)

    theirs = lax.ppermute(half, "core", SWAP)
    late_tokens, _ = lax.optimization_barrier((tokens, half))
    high = stage(late_tokens, STAGED, tokens.shape[1] - STAGED)

    delta, given = give(core, half, theirs, cot, low, high)
    got = lax.ppermute(given, "core", SWAP)
    kept = keep(core, delta, low, high)

    from_x = lax.all_to_all(
        add(kept, got), ("y_lo", "x"), split_axis=0, concat_axis=0, tiled=True
    )
    by_yz = sum_peers(from_x).reshape(Z_LO * Y_HI * Z_HI, PIECE_BLOCKS, BLOCK)
    from_yz = lax.all_to_all(
        by_yz, ("z_lo", "y_hi", "z_hi"), split_axis=0, concat_axis=0, tiled=True
    )
    return final_sum(from_yz)


def solution(mesh):
    fine = Mesh(
        mesh.devices.reshape(Z_LO, Y_HI, Y_LO, CORE, Z_HI, X),
        ("z_lo", "y_hi", "y_lo", "core", "z_hi", "x"),
    )
    outer, inner = ("z_lo", "y_hi", "y_lo", "core"), ("z_hi", "x")
    in_specs = (
        P(outer + inner, None),
        P(outer + inner, None),
        P(None, inner, None),
        P(None, inner),
    )
    return jax.shard_map(
        on_device, mesh=fine, in_specs=in_specs, out_specs=P(outer + inner, None), check_vma=False
    )
```
